32 devices in a mesh: grp: 2 (over y), zone: 4 (over x, core), tile: 4 (over z).
Axes of the slice: x: 2, y: 2, z: 4, core: 2. Of those that a mesh axis runs over, the one named last changes fastest.
Arguments:
- mask_levels: int32 [8, 512, 512], P(('grp', 'tile')), parts along dimension 0, may hold values from 0 to 15
- blend_weights: int32 [8, 512], P(('grp', 'tile')), parts along dimension 0, may hold values from 0 to 16
- zone_pairs: int32 [8, 2], P('grp'), parts along dimension 0, may hold values from 0 to 3, as said below
- kernels: bfloat16 [4, 4, 2, 512, 512], P(None, 'zone', None, 'tile'), may hold values from -6 to 6
- resist_cot: float32 [8, 512, 512], P(('grp', 'tile')), parts along dimension 0, may hold values from -6 to 6
Outputs:
- mask_grad: float32 [8, 512, 512], P(('grp', 'tile'), 'zone'), parts along dimension 0
- kernel_grad: float32 [8, 4, 2, 512, 512], P('grp', 'zone', None, 'tile'), parts along dimension 0
The draws below stay inside these ranges and needn't reach their ends.
There are 2 independent parts, one for each index of `grp`. The reference program is written for one: setup_inputs(seed, part) draws one part's arguments, and reference() takes and returns one part's arrays. A program takes and returns all parts, laid end to end along the dimension named above; an argument that names none is the same for every part. Nothing has to cross between parts.
Inputs may be any that keep to these rules, and one draw needn't show every extreme that they name: `zone_pairs`: column 0 lists the 4 zones in some order, each once; in each row, column 1 is either the same zone as column 0 or the next zone after it, where the zone after zone 3 is zone 0.
All inputs are finite; a program needn't handle non-finite values.
Results may differ from the reference program's by a relative error of at most 0.017.
The reference program's roundings to bfloat16 on the way count: a program that leaves them out, or rounds other values in their place, can miss the bound.
Values may be sent and summed in bfloat16 or wider, within the bound.
A program may use at most 128 MiB of HBM per device.

```python
import math
import jax
import jax.numpy as jnp
from jax import lax

P_SIZE = 512
KDEV = 1
LEVELS = 15
BLEND = 16
KERN = 4
TILES = 4
ZONES = 4
N_ZONE = 4


def draw_zone_pairs(key, part):
    key = jax.random.fold_in(key, 7)
    first_key, second_key = jax.random.split(key)
    first_zone = jax.random.permutation(first_key, ZONES).astype(jnp.int32)
    offset = jax.random.randint(second_key, (TILES,), 0, 2).astype(jnp.int32)
    second_zone = (first_zone + offset) % ZONES
    return jnp.stack([first_zone, second_zone], axis=1)


def with_ends(values, own_key, low, top_value):
    shape = values.shape
    place = [jax.random.randint(jax.random.fold_in(own_key, axis), (), 0, shape[axis]) for axis in range(len(shape))]
    values = values.at[tuple(place)].set(low)
    longest = shape.index(max(shape))
    place[longest] = (place[longest] + 1) % shape[longest]
    return values.at[tuple(place)].set(top_value)


def shard_levels(stream_key, shape, pieces, least, largest):
    def one(axis_at, parts):
        heights = jax.random.uniform(jax.random.fold_in(jax.random.fold_in(stream_key, 6), axis_at), (parts,), jnp.float32, least / len(pieces), largest / len(pieces))
        return jnp.repeat(jnp.exp(heights), shape[axis_at] // parts).reshape((-1,) + (1,) * (len(shape) - axis_at - 1))

    level = one(*pieces[0])
    for cut in pieces[1:]:
        level = level * one(*cut)
    return level


def centred(key, dims, width, most, pieces=(), kind=jnp.bfloat16):
    loudness = shard_levels(key, dims, pieces, -0.22, 0.18) if pieces else 1.0
    drawn = jax.random.normal(key, dims, jnp.float32) * width * loudness
    return jnp.minimum(jnp.maximum(drawn, -most), most).astype(kind)


def setup_inputs(seed: int = 0, part: int = 0) -> dict:
    key_of = jax.random.split(jax.random.key(seed), 6)
    part_splits = jax.random.split(jax.random.fold_in(key_of[5], part), 6)
    mask_levels = with_ends(jax.random.randint(part_splits[0], (TILES, P_SIZE, P_SIZE), 0, LEVELS + 1), jax.random.fold_in(part_splits[0], 1), 0, LEVELS).astype(jnp.int32)
    blend_weights = with_ends(jax.random.randint(part_splits[1], (TILES, P_SIZE), 0, BLEND + 1), jax.random.fold_in(part_splits[1], 1), 0, BLEND).astype(jnp.int32)
    zone_pairs = draw_zone_pairs(jax.random.fold_in(jax.random.fold_in(key_of[5], part), 71), part)
    kernels = centred(key_of[3], (ZONES, KERN, 2, P_SIZE, P_SIZE), ((1.32 / KERN) ** 0.5), 6.0, ((1, 4), (3, 4)))
    resist_cot = centred(part_splits[4], (TILES, P_SIZE, P_SIZE), 1.0, 6.0, ((0, 4),), jnp.float32)
    return {"mask_levels": mask_levels, "blend_weights": blend_weights, "zone_pairs": zone_pairs, "kernels": kernels, "resist_cot": resist_cot}


steepness = 4.0
threshold = 1.0

def dft_tables(length):
    index_row = jnp.arange(length, dtype=jnp.int32)
    phase = index_row[:, None] * index_row[None, :] % length
    angle = phase.astype(jnp.float32) * (2.0 * math.pi / length)
    factor = 1.0 / math.sqrt(length)
    return ((jnp.cos(angle) * factor).astype(jnp.bfloat16), (-jnp.sin(angle) * factor).astype(jnp.bfloat16))

def product(left, right):
    return jnp.dot(left, right, preferred_element_type=jnp.float32)

def spectrum(mask_value, cos_table, sin_table):
    left_re = product(cos_table, mask_value).astype(jnp.bfloat16)
    left_im = product(sin_table, mask_value).astype(jnp.bfloat16)
    spec_re = product(left_re, cos_table) - product(left_im, sin_table)
    spec_im = product(left_re, sin_table) + product(left_im, cos_table)
    return (spec_re, spec_im)

def image_field(kernel_re, kernel_im, spec_re, spec_im, cos_table, sin_table):
    kern_re = kernel_re.astype(jnp.float32)
    kern_im = kernel_im.astype(jnp.float32)
    wave_re = (kern_re * spec_re - kern_im * spec_im).astype(jnp.bfloat16)
    wave_im = (kern_re * spec_im + kern_im * spec_re).astype(jnp.bfloat16)
    half_re = (product(cos_table, wave_re) + product(sin_table, wave_im)).astype(jnp.bfloat16)
    half_im = (product(cos_table, wave_im) - product(sin_table, wave_re)).astype(jnp.bfloat16)
    field_re = product(half_re, cos_table) + product(half_im, sin_table)
    field_im = product(half_im, cos_table) - product(half_re, sin_table)
    return (field_re, field_im)

def field_grad(kernel_re, kernel_im, field_re, field_im, scaled, spec_re, spec_im, cos_table, sin_table):
    grad_re = (scaled * field_re).astype(jnp.bfloat16)
    grad_im = (scaled * field_im).astype(jnp.bfloat16)
    half_re = (product(cos_table, grad_re) - product(sin_table, grad_im)).astype(jnp.bfloat16)
    half_im = (product(cos_table, grad_im) + product(sin_table, grad_re)).astype(jnp.bfloat16)
    wave_re = product(half_re, cos_table) - product(half_im, sin_table)
    wave_im = product(half_re, sin_table) + product(half_im, cos_table)
    kern_re = kernel_re.astype(jnp.float32)
    kern_im = kernel_im.astype(jnp.float32)
    kgrad_re = wave_re * spec_re + wave_im * spec_im
    kgrad_im = wave_im * spec_re - wave_re * spec_im
    sgrad_re = wave_re * kern_re + wave_im * kern_im
    sgrad_im = wave_im * kern_re - wave_re * kern_im
    return (jnp.stack([kgrad_re, kgrad_im]), sgrad_re, sgrad_im)

def slot_forward(panel_slot, spec, tables):
    return jax.vmap(image_field, (0, 0, None, None, None, None))(panel_slot[:, 0], panel_slot[:, 1], spec[0], spec[1], tables[0], tables[1])

def energy(fields):
    return lax.optimization_barrier(jnp.sum(fields[0] * fields[0] + fields[1] * fields[1], axis=0))

def slot_backward(panel_slot, fields, scaled, spec, tables):
    kgrad, sgrad_re, sgrad_im = jax.vmap(field_grad, (0, 0, 0, 0, None, None, None, None, None))(panel_slot[:, 0], panel_slot[:, 1], fields[0], fields[1], scaled, spec[0], spec[1], tables[0], tables[1])
    return (kgrad, lax.optimization_barrier(jnp.sum(sgrad_re, axis=0)), lax.optimization_barrier(jnp.sum(sgrad_im, axis=0)))

def mask_back(sgrad_re, sgrad_im, cos_table, sin_table):
    half_re = (product(cos_table, sgrad_re) + product(sin_table, sgrad_im)).astype(jnp.bfloat16)
    half_im = (product(cos_table, sgrad_im) - product(sin_table, sgrad_re)).astype(jnp.bfloat16)
    return product(half_re, cos_table) + product(half_im, sin_table)

def resist_slope(intensity, cotangent):
    resist = jax.nn.sigmoid(steepness * (intensity - threshold))
    return cotangent * steepness * resist * (1.0 - resist)

def reference(mask_levels, blend_weights, zone_pairs, kernels, resist_cot):
    length = mask_levels.shape[2]
    tables = dft_tables(length)

    def one_tile(grad_total, tile_items):
        levels, blend_row, zone_pair, cotangent = tile_items
        mask_value = (2.0 * levels.astype(jnp.float32) / LEVELS - 1.0).astype(jnp.bfloat16)
        spec = spectrum(mask_value, tables[0], tables[1])
        is_seam = zone_pair[0] != zone_pair[1]
        share = jnp.where(is_seam, blend_row.astype(jnp.float32) / BLEND, jnp.float32(1.0))
        shares = (share, 1.0 - share)
        panels = jnp.take(kernels, zone_pair, axis=0)
        forward = []
        summed = jnp.zeros((length, length), jnp.float32)
        for group_index in range(N_ZONE):
            lower = group_index * KDEV
            first = slot_forward(panels[0, lower:lower + KDEV], spec, tables)
            second = slot_forward(panels[1, lower:lower + KDEV], spec, tables)
            forward.append((first, second))
            summed = summed + (shares[0][None, :] * energy(first) + shares[1][None, :] * energy(second))
        slope = resist_slope(summed, cotangent)
        mask_total = jnp.zeros((length, length), jnp.float32)
        grads_first = []
        grads_second = []
        for group_index in range(N_ZONE):
            lower = group_index * KDEV
            first, second = forward[group_index]
            back_first = slot_backward(panels[0, lower:lower + KDEV], first, 2.0 * shares[0][None, :] * slope, spec, tables)
            back_second = slot_backward(panels[1, lower:lower + KDEV], second, 2.0 * shares[1][None, :] * slope, spec, tables)
            sgrad_re = (back_first[1] + back_second[1]).astype(jnp.bfloat16)
            sgrad_im = (back_first[2] + back_second[2]).astype(jnp.bfloat16)
            mask_total = mask_total + mask_back(sgrad_re, sgrad_im, tables[0], tables[1])
            grads_first.append(back_first[0])
            grads_second.append(back_second[0])
        grad_total = grad_total.at[zone_pair[0]].add(jnp.concatenate(grads_first, axis=0))
        grad_total = grad_total.at[zone_pair[1]].add(jnp.concatenate(grads_second, axis=0))
        return (grad_total, mask_total)
    start_grad = jnp.zeros(kernels.shape, jnp.float32)
    grad_total, mask_grads = lax.scan(one_tile, start_grad, (mask_levels, blend_weights, zone_pairs, resist_cot))
    return (mask_grads, grad_total)
```

```python
import functools
import math

import jax
import jax.numpy as jnp
import ml_dtypes
import numpy as np
from jax import lax
from jax.experimental import pallas as pl
from jax.experimental.pallas import tpu as pltpu
from jax.sharding import PartitionSpec as P

LEVELS = 15
BLEND = 16
STEEP = 4.0
THRESHOLD = 1.0
F32 = jnp.float32
BF16 = jnp.bfloat16
MESH = pl.DeviceIdType.MESH
CORES = 2


def stacked_tables(length):
    index = np.arange(length, dtype=np.int64)
    angle = ((index[:, None] * index[None, :]) % length) * (2.0 * math.pi / length)
    factor = 1.0 / math.sqrt(length)
    cos = (np.cos(angle) * factor).astype(np.float32).astype(ml_dtypes.bfloat16)
    sin = (-np.sin(angle) * factor).astype(np.float32).astype(ml_dtypes.bfloat16)
    back = np.block([[cos, sin], [-sin, cos]]).astype(ml_dtypes.bfloat16)
    fore = np.block([[cos, -sin], [sin, cos]]).astype(ml_dtypes.bfloat16)
    return back, fore


def dot(left, right):
    return jnp.dot(left, right, preferred_element_type=F32)


def blocks(total, step, body):
    def one(index, carry):
        body(pl.multiple_of(index * step, step))
        return carry

    lax.fori_loop(0, total // step, one, 0)


def kernel(
    sizes,
    pairs,
    blend,
    kern,
    levels_any,
    cot_any,
    back_any,
    fore_any,
    mask_out,
    kgrad_out,
    levels,
    cot,
    back,
    fore,
    outgoing,
    panels,
    mvals,
    left,
    spec,
    wave,
    fields,
    image,
    sib_in,
    chip_sum,
    chip_in,
    slope,
    kg_send,
    kg_recv,
    ygrad,
    ystack,
    mk_own,
    mk_send,
    mk_recv,
    local_sem,
    pan_s,
    pan_r,
    sib_s,
    sib_r,
    chip_s,
    chip_r,
    slope_s,
    slope_r,
    kg_s,
    kg_r,
    mk_s,
    mk_r,
):
    tiles, zdev, length, rows, zones = sizes
    n = length
    step = n // 2
    zrows = n // zdev
    chips = zdev // CORES
    me_t = lax.axis_index("tile")
    me_z = lax.axis_index("zone")
    chip = me_z // CORES
    core = me_z % CORES
    sib = chip * CORES + (1 - core)

    loads = [
        pltpu.make_async_copy(src, dst, local_sem.at[i])
        for i, (src, dst) in enumerate(
            ((levels_any, levels), (back_any, back), (fore_any, fore), (cot_any, cot))
        )
    ]
    barrier = pltpu.get_barrier_semaphore()
    for d in range(1, tiles):
        pl.semaphore_signal(
            barrier, inc=1, device_id={"tile": lax.rem(me_t + d, tiles)}, device_id_type=MESH
        )
    for d in range(1, zdev):
        pl.semaphore_signal(
            barrier, inc=1, device_id={"zone": lax.rem(me_z + d, zdev)}, device_id_type=MESH
        )
    my_rows = pl.ds(pl.multiple_of(me_t * rows, rows), rows)
    for t in range(tiles):
        for s in range(2):
            outgoing[t, s] = kern[pairs[t, s], 0]
    for s in range(2):
        panels[s, :, my_rows, :] = kern[pairs[me_t, s], 0]
    pl.semaphore_wait(barrier, tiles + zdev - 2)

    def panel_copy(s, d):
        peer = lax.rem(me_t + d, tiles)
        return pltpu.make_async_remote_copy(
            src_ref=outgoing.at[peer, s],
            dst_ref=panels.at[s, :, my_rows, :],
            send_sem=pan_s.at[s, d - 1],
            recv_sem=pan_r.at[s, d - 1],
            device_id={"tile": peer},
            device_id_type=MESH,
        )

    for s in range(2):
        for d in range(tiles - 1, 0, -1):
            panel_copy(s, d).start()
    for load in loads:
        load.start()

    first_zone, second_zone = pairs[me_t, 0], pairs[me_t, 1]
    share0 = jnp.where(first_zone != second_zone, blend[...].astype(F32) / BLEND, F32(1.0))
    shares = (share0, 1.0 - share0)

    loads[0].wait()
    mvals[...] = (2.0 * levels[...].astype(F32) / LEVELS - 1.0).astype(BF16)
    loads[1].wait()
    loads[2].wait()
    for h in range(2):

        def stage(r, h=h):
            left[pl.ds(r, step), h * n : (h + 1) * n] = dot(
                fore[pl.ds(h * n + r, step), :n], mvals[...]
            ).astype(BF16)

        blocks(n, step, stage)

    def stage(r):
        spec[pl.ds(r, step), :] = dot(left[pl.ds(r, step), :], back[...])

    blocks(n, step, stage)

    def from_left(table, h):
        def stage(r):
            left[pl.ds(r, step), h * n : (h + 1) * n] = dot(
                table[pl.ds(h * n + r, step), :], wave[...]
            ).astype(BF16)

        blocks(n, step, stage)

    for s in range(2):
        for d in range(1, tiles):
            panel_copy(s, d).wait_recv()

        def stage(r, s=s):
            at = pl.ds(r, 64)
            hr, hi = panels[s, 0, at, :].astype(F32), panels[s, 1, at, :].astype(F32)
            sr, si = spec[at, :n], spec[at, n:]
            wave[at, :] = (hr * sr - hi * si).astype(BF16)
            wave[pl.ds(n + r, 64), :] = (hr * si + hi * sr).astype(BF16)

        blocks(n, 64, stage)
        from_left(back, 0)
        from_left(back, 1)

        def stage(r, s=s):
            at = pl.ds(r, step)
            e = dot(left[at, :], fore[...])
            fields[s, at, :] = e
            er, ei = e[:, :n], e[:, n:]
            term = shares[s] * (er * er + ei * ei)
            image[at, :] = term if s == 0 else image[at, :] + term

        blocks(n, step, stage)

    half = n // CORES
    mine = pl.ds(pl.multiple_of(core * half, half), half)
    other = pl.ds(pl.multiple_of((1 - core) * half, half), half)
    to_sib = pltpu.make_async_remote_copy(
        src_ref=image.at[other, :],
        dst_ref=sib_in,
        send_sem=sib_s,
        recv_sem=sib_r,
        device_id={"zone": sib},
        device_id_type=MESH,
    )
    to_sib.start()
    to_sib.wait_recv()
    chip_sum[...] = image[mine, :] + sib_in[...]

    def chip_copy(d):
        return pltpu.make_async_remote_copy(
            src_ref=chip_sum,
            dst_ref=chip_in.at[d - 1],
            send_sem=chip_s.at[d - 1],
            recv_sem=chip_r.at[d - 1],
            device_id={"zone": lax.rem(chip + d, chips) * CORES + core},
            device_id_type=MESH,
        )

    for d in range(1, chips):
        chip_copy(d).start()
    loads[3].wait()
    for d in range(1, chips):
        chip_copy(d).wait_recv()

    def stage(r):
        at = pl.ds(r, 64)
        total = chip_sum[at, :]
        for d in range(1, chips):
            total = total + chip_in[d - 1, at, :]
        resist = jax.nn.sigmoid(STEEP * (total - THRESHOLD))
        here = pl.ds(pl.multiple_of(core * half + r, 64), 64)
        slope[here, :] = cot[here, :] * STEEP * resist * (1.0 - resist)

    blocks(half, 64, stage)
    slope_copy = pltpu.make_async_remote_copy(
        src_ref=slope.at[mine, :],
        dst_ref=slope.at[mine, :],
        send_sem=slope_s,
        recv_sem=slope_r,
        device_id={"zone": sib},
        device_id_type=MESH,
    )
    slope_copy.start()
    slope_copy.wait_recv()

    def kg_copy(s, d):
        peer = lax.rem(me_t + d, tiles)
        return pltpu.make_async_remote_copy(
            src_ref=kg_send.at[peer, s],
            dst_ref=kg_recv.at[me_t, s],
            send_sem=kg_s.at[s, d - 1],
            recv_sem=kg_r.at[s, d - 1],
            device_id={"tile": peer},
            device_id_type=MESH,
        )

    for s in range(2):

        def stage(r, s=s):
            at = pl.ds(r, 64)
            scaled = 2.0 * shares[s] * slope[at, :]
            wave[at, :] = (scaled * fields[s, at, :n]).astype(BF16)
            wave[pl.ds(n + r, 64), :] = (scaled * fields[s, at, n:]).astype(BF16)

        blocks(n, 64, stage)
        from_left(fore, 0)
        from_left(fore, 1)

        def rows_of(peer, s=s):
            base = pl.multiple_of(peer * rows, rows)
            at = pl.ds(base, rows)
            v = dot(left[at, :], back[...])
            vr, vi = v[:, :n], v[:, n:]
            sr, si = spec[at, :n], spec[at, n:]
            hr, hi = panels[s, 0, at, :].astype(F32), panels[s, 1, at, :].astype(F32)
            yr = vr * hr + vi * hi
            yi = vi * hr - vr * hi
            if s == 0:
                ygrad[at, :n] = yr
                ygrad[at, n:] = yi
            else:
                ystack[at, :] = (ygrad[at, :n] + yr).astype(BF16)
                ystack[pl.ds(n + base, rows), :] = (ygrad[at, n:] + yi).astype(BF16)
            return (vr * sr + vi * si).astype(BF16), (vi * sr - vr * si).astype(BF16)

        def away(i, carry, s=s):
            d = tiles - 1 - i
            peer = lax.rem(me_t + d, tiles)
            re, im = rows_of(peer)
            kg_send[peer, s, 0] = re
            kg_send[peer, s, 1] = im
            kg_copy(s, d).start()
            return carry

        lax.fori_loop(0, tiles - 1, away, 0)
        re, im = rows_of(me_t)
        kg_recv[me_t, s, 0] = re
        kg_recv[me_t, s, 1] = im

    for h in range(2):

        def stage(r, h=h):
            left[pl.ds(r, step), h * n : (h + 1) * n] = dot(
                back[pl.ds(h * n + r, step), :], ystack[...]
            ).astype(BF16)

        blocks(n, step, stage)

    def mk_copy(d):
        peer = lax.rem(me_z + d, zdev)
        return pltpu.make_async_remote_copy(
            src_ref=mk_send.at[peer],
            dst_ref=mk_recv.at[d - 1],
            send_sem=mk_s.at[d - 1],
            recv_sem=mk_r.at[d - 1],
            device_id={"zone": peer},
            device_id_type=MESH,
        )

    def mask_rows(peer):
        return dot(left[pl.ds(pl.multiple_of(peer * zrows, zrows), zrows), :], fore[:, :n])

    def away(i, carry):
        d = i + 1
        peer = lax.rem(me_z + d, zdev)
        mk_send[peer] = mask_rows(peer).astype(BF16)
        mk_copy(d).start()
        return carry

    lax.fori_loop(0, zdev - 1, away, 0)
    mk_own[...] = mask_rows(me_z)
    total = mk_own[...]
    for d in range(1, zdev):
        mk_copy(d).wait_recv()
        total = total + mk_recv[d - 1].astype(F32)
    mask_out[...] = total

    owners = []
    for z in range(zones):
        owner = jnp.int32(0)
        for t in range(tiles):
            owner = jnp.where(pairs[t, 0] == z, jnp.int32(t), owner)
        owners.append(owner)
    for s in range(2):
        for d in range(1, tiles):
            kg_copy(s, d).wait_recv()
    for z in range(zones):
        own, prior = owners[z], owners[(z - 1) % zones]
        keep_own = pairs[own, 1] == pairs[own, 0]
        keep_prior = pairs[prior, 1] != pairs[prior, 0]
        value = kg_recv[own, 0].astype(F32)
        value = value + jnp.where(keep_own, kg_recv[own, 1].astype(F32), 0.0)
        value = value + jnp.where(keep_prior, kg_recv[prior, 1].astype(F32), 0.0)
        kgrad_out[z, 0] = value

    for s in range(2):
        for d in range(1, tiles):
            panel_copy(s, d).wait_send()
            kg_copy(s, d).wait_send()
    to_sib.wait_send()
    slope_copy.wait_send()
    for d in range(1, chips):
        chip_copy(d).wait_send()
    for d in range(1, zdev):
        mk_copy(d).wait_send()


def shards(sizes, mask_levels, blend_weights, zone_pairs, kernels, resist_cot):
    tiles, zdev, n, rows, zones = sizes
    back, fore = stacked_tables(n)
    zrows = n // zdev
    chips = zdev // CORES
    half = n // CORES
    vmem = pl.BlockSpec(memory_space=pltpu.VMEM)
    anywhere = pl.BlockSpec(memory_space=pl.ANY)
    dma = pltpu.SemaphoreType.DMA
    away = max(tiles - 1, 1)
    mask_grad, kernel_grad = pl.pallas_call(
        functools.partial(kernel, sizes),
        out_shape=(
            jax.ShapeDtypeStruct((zrows, n), F32),
            jax.ShapeDtypeStruct((zones, 1, 2, rows, n), F32),
        ),
        in_specs=[
            pl.BlockSpec(memory_space=pltpu.SMEM),
            vmem,
            vmem,
            anywhere,
            anywhere,
            anywhere,
            anywhere,
        ],
        out_specs=(vmem, vmem),
        scratch_shapes=[
            pltpu.VMEM((n, n), jnp.int32),
            pltpu.VMEM((n, n), F32),
            pltpu.VMEM((2 * n, 2 * n), BF16),
            pltpu.VMEM((2 * n, 2 * n), BF16),
            pltpu.VMEM((tiles, 2, 2, rows, n), BF16),
            pltpu.VMEM((2, 2, n, n), BF16),
            pltpu.VMEM((n, n), BF16),
            pltpu.VMEM((n, 2 * n), BF16),
            pltpu.VMEM((n, 2 * n), F32),
            pltpu.VMEM((2 * n, n), BF16),
            pltpu.VMEM((2, n, 2 * n), F32),
            pltpu.VMEM((n, n), F32),
            pltpu.VMEM((half, n), F32),
            pltpu.VMEM((half, n), F32),
            pltpu.VMEM((chips - 1, half, n), F32),
            pltpu.VMEM((n, n), F32),
            pltpu.VMEM((tiles, 2, 2, rows, n), BF16),
            pltpu.VMEM((tiles, 2, 2, rows, n), BF16),
            pltpu.VMEM((n, 2 * n), F32),
            pltpu.VMEM((2 * n, n), BF16),
            pltpu.VMEM((zrows, n), F32),
            pltpu.VMEM((zdev, zrows, n), BF16),
            pltpu.VMEM((zdev - 1, zrows, n), BF16),
            dma((4,)),
            dma((2, away)),
            dma((2, away)),
            dma,
            dma,
            dma((chips - 1,)),
            dma((chips - 1,)),
            dma,
            dma,
            dma((2, away)),
            dma((2, away)),
            dma((zdev - 1,)),
            dma((zdev - 1,)),
        ],
        compiler_params=pltpu.CompilerParams(
            collective_id=0, has_side_effects=True, vmem_limit_bytes=56 * 1024 * 1024
        ),
        cost_estimate=pl.CostEstimate(
            flops=88 * n * n * n, bytes_accessed=10 * n * n * 4, transcendentals=n * n
        ),
    )(
        zone_pairs,
        blend_weights,
        kernels,
        mask_levels[0],
        resist_cot[0],
        jnp.asarray(back),
        jnp.asarray(fore),
    )
    return (mask_grad[None], kernel_grad)


def solution(mesh):
    placed = (
        P(("grp", "tile"), None, None),
        P(("grp", "tile"), None),
        P("grp", None),
        P(None, "zone", None, "tile", None),
        P(("grp", "tile"), None, None),
    )

    def run(mask_levels, blend_weights, zone_pairs, kernels, resist_cot):
        tiles, zdev = mesh.shape["tile"], mesh.shape["zone"]
        sizes = (
            tiles,
            zdev,
            mask_levels.shape[2],
            kernels.shape[3] // tiles,
            kernels.shape[0],
        )
        return jax.shard_map(
            functools.partial(shards, sizes),
            mesh=mesh,
            in_specs=placed,
            out_specs=(P(("grp", "tile"), "zone", None), P("grp", "zone", None, "tile", None)),
            check_vma=False,
        )(mask_levels, blend_weights, zone_pairs, kernels, resist_cot)

    return run
```

```python
import functools
import math

import jax
import jax.numpy as jnp
import ml_dtypes
import numpy as np
from jax import lax
from jax.experimental import pallas as pl
from jax.experimental.pallas import tpu as pltpu
from jax.sharding import PartitionSpec as P

LEVELS = 15
BLEND = 16
STEEP = 4.0
THRESHOLD = 1.0
F32 = jnp.float32
BF16 = jnp.bfloat16
MESH = pl.DeviceIdType.MESH
PIECES = 4
CORES = 2


def stacked_tables(length):
    index = np.arange(length, dtype=np.int64)
    angle = ((index[:, None] * index[None, :]) % length) * (2.0 * math.pi / length)
    factor = 1.0 / math.sqrt(length)
    cos = (np.cos(angle) * factor).astype(np.float32).astype(ml_dtypes.bfloat16)
    sin = (-np.sin(angle) * factor).astype(np.float32).astype(ml_dtypes.bfloat16)
    back = np.block([[cos, sin], [-sin, cos]]).astype(ml_dtypes.bfloat16)
    fore = np.block([[cos, -sin], [sin, cos]]).astype(ml_dtypes.bfloat16)
    return back, fore


def dot(left, right):
    return jnp.dot(left, right, preferred_element_type=F32)


def blocks(total, step, body):
    def one(index, carry):
        body(pl.multiple_of(index * step, step))
        return carry

    lax.fori_loop(0, total // step, one, 0)


def kernel(
    sizes,
    pairs,
    blend,
    kern,
    levels_any,
    cot_any,
    back_any,
    fore_any,
    mask_out,
    kg_out,
    levels,
    cot,
    back,
    fore,
    outgoing,
    panels,
    mvals,
    left,
    spec,
    wave,
    fields,
    image,
    sib_in,
    chip_sum,
    chip_send,
    chip_in,
    slope,
    kg_send,
    kg_recv,
    ygrad,
    ystack,
    mk_own,
    mk_send,
    mk_recv,
    local_sem,
    pan_s,
    pan_r,
    sib_s,
    sib_r,
    chip_s,
    chip_r,
    slope_s,
    slope_r,
    kg_s,
    kg_r,
    mk_s,
    mk_r,
    out_sem,
):
    tiles, zdev, length, rows, zones = sizes
    n = length
    step = n // 2
    zrows = n // zdev
    chips = zdev // CORES
    me_t = lax.axis_index("tile")
    me_z = lax.axis_index("zone")
    chip = me_z // CORES
    core = me_z % CORES
    sib = chip * CORES + (1 - core)

    loads = [
        pltpu.make_async_copy(src, dst, local_sem.at[i])
        for i, (src, dst) in enumerate(
            ((levels_any, levels), (back_any, back), (fore_any, fore), (cot_any, cot))
        )
    ]
    barrier = pltpu.get_barrier_semaphore()
    for d in range(1, tiles):
        pl.semaphore_signal(
            barrier, inc=1, device_id={"tile": lax.rem(me_t + d, tiles)}, device_id_type=MESH
        )
    for d in range(1, zdev):
        pl.semaphore_signal(
            barrier, inc=1, device_id={"zone": lax.rem(me_z + d, zdev)}, device_id_type=MESH
        )
    my_rows = pl.ds(pl.multiple_of(me_t * rows, rows), rows)
    for t in range(tiles):
        for s in range(2):
            outgoing[t, s] = kern[pairs[t, s], 0]
    for s in range(2):
        panels[s, :, my_rows, :] = kern[pairs[me_t, s], 0]
    pl.semaphore_wait(barrier, tiles + zdev - 2)

    def panel_copy(s, d):
        peer = lax.rem(me_t + d, tiles)
        return pltpu.make_async_remote_copy(
            src_ref=outgoing.at[peer, s],
            dst_ref=panels.at[s, :, my_rows, :],
            send_sem=pan_s.at[s, d - 1],
            recv_sem=pan_r.at[s, d - 1],
            device_id={"tile": peer},
            device_id_type=MESH,
        )

    for s in range(2):
        for d in range(tiles - 1, 0, -1):
            panel_copy(s, d).start()
    for load in loads:
        load.start()

    first_zone, second_zone = pairs[me_t, 0], pairs[me_t, 1]
    share0 = jnp.where(first_zone != second_zone, blend[...].astype(F32) / BLEND, F32(1.0))
    shares = (share0, 1.0 - share0)

    loads[0].wait()
    mvals[...] = (2.0 * levels[...].astype(F32) / LEVELS - 1.0).astype(BF16)
    loads[1].wait()
    loads[2].wait()
    for h in range(2):

        def stage(r, h=h):
            left[pl.ds(r, step), h * n : (h + 1) * n] = dot(
                fore[pl.ds(h * n + r, step), :n], mvals[...]
            ).astype(BF16)

        blocks(n, step, stage)

    def stage(r):
        spec[pl.ds(r, step), :] = dot(left[pl.ds(r, step), :], back[...])

    blocks(n, step, stage)

    def from_left(table, h):
        def stage(r):
            left[pl.ds(r, step), h * n : (h + 1) * n] = dot(
                table[pl.ds(h * n + r, step), :], wave[...]
            ).astype(BF16)

        blocks(n, step, stage)

    half = n // CORES
    piece = half // PIECES
    to_sib = pltpu.make_async_remote_copy(
        src_ref=image.at[pl.ds(pl.multiple_of((1 - core) * half, half), half), :],
        dst_ref=sib_in,
        send_sem=sib_s,
        recv_sem=sib_r,
        device_id={"zone": sib},
        device_id_type=MESH,
    )

    for s in range(2):
        for d in range(1, tiles):
            panel_copy(s, d).wait_recv()

        def stage(r, s=s):
            at = pl.ds(r, 64)
            hr, hi = panels[s, 0, at, :].astype(F32), panels[s, 1, at, :].astype(F32)
            sr, si = spec[at, :n], spec[at, n:]
            wave[at, :] = (hr * sr - hi * si).astype(BF16)
            wave[pl.ds(n + r, 64), :] = (hr * si + hi * sr).astype(BF16)

        blocks(n, 64, stage)
        from_left(back, 0)
        from_left(back, 1)

        for i in range(CORES):
            start = (1 - core) * half if i == 0 else core * half
            at = pl.ds(pl.multiple_of(start, half), half)
            e = dot(left[at, :], fore[...])
            fields[s, at, :] = e
            er, ei = e[:, :n], e[:, n:]
            term = shares[s] * (er * er + ei * ei)
            image[at, :] = term if s == 0 else image[at, :] + term
            if s == 1 and i == 0:
                to_sib.start()

    to_sib.wait_recv()

    def chip_copy(d, p):
        at = pl.ds(p * piece, piece)
        return pltpu.make_async_remote_copy(
            src_ref=chip_send.at[at, :],
            dst_ref=chip_in.at[d - 1, at, :],
            send_sem=chip_s.at[d - 1, p],
            recv_sem=chip_r.at[d - 1, p],
            device_id={"zone": lax.rem(chip + d, chips) * CORES + core},
            device_id_type=MESH,
        )

    for p in range(PIECES):
        at = pl.ds(p * piece, piece)
        here = pl.ds(pl.multiple_of(core * half + p * piece, piece), piece)
        total = image[here, :] + sib_in[at, :]
        chip_sum[at, :] = total
        chip_send[at, :] = total.astype(BF16)
        for d in range(1, chips):
            chip_copy(d, p).start()
    loads[3].wait()

    def slope_copy(p):
        here = pl.ds(pl.multiple_of(core * half + p * piece, piece), piece)
        return pltpu.make_async_remote_copy(
            src_ref=slope.at[here, :],
            dst_ref=slope.at[here, :],
            send_sem=slope_s.at[p],
            recv_sem=slope_r.at[p],
            device_id={"zone": sib},
            device_id_type=MESH,
        )

    for p in range(PIECES):
        for d in range(1, chips):
            chip_copy(d, p).wait_recv()
        at = pl.ds(p * piece, piece)
        total = chip_sum[at, :]
        for d in range(1, chips):
            total = total + chip_in[d - 1, at, :].astype(F32)
        resist = jax.nn.sigmoid(STEEP * (total - THRESHOLD))
        here = pl.ds(pl.multiple_of(core * half + p * piece, piece), piece)
        slope[here, :] = cot[here, :] * STEEP * resist * (1.0 - resist)
        slope_copy(p).start()
    for p in range(PIECES):
        slope_copy(p).wait_recv()

    def kg_copy(s, d):
        peer = lax.rem(me_t + d, tiles)
        return pltpu.make_async_remote_copy(
            src_ref=kg_send.at[peer, s],
            dst_ref=kg_recv.at[me_t, s],
            send_sem=kg_s.at[s, d - 1],
            recv_sem=kg_r.at[s, d - 1],
            device_id={"tile": peer},
            device_id_type=MESH,
        )

    for s in range(2):

        def stage(r, s=s):
            at = pl.ds(r, 64)
            scaled = 2.0 * shares[s] * slope[at, :]
            wave[at, :] = (scaled * fields[s, at, :n]).astype(BF16)
            wave[pl.ds(n + r, 64), :] = (scaled * fields[s, at, n:]).astype(BF16)

        blocks(n, 64, stage)
        from_left(fore, 0)
        from_left(fore, 1)

        def rows_of(peer, s=s):
            base = pl.multiple_of(peer * rows, rows)
            at = pl.ds(base, rows)
            v = dot(left[at, :], back[...])
            vr, vi = v[:, :n], v[:, n:]
            sr, si = spec[at, :n], spec[at, n:]
            hr, hi = panels[s, 0, at, :].astype(F32), panels[s, 1, at, :].astype(F32)
            yr = vr * hr + vi * hi
            yi = vi * hr - vr * hi
            if s == 0:
                ygrad[at, :n] = yr
                ygrad[at, n:] = yi
            else:
                ystack[at, :] = (ygrad[at, :n] + yr).astype(BF16)
                ystack[pl.ds(n + base, rows), :] = (ygrad[at, n:] + yi).astype(BF16)
            return (vr * sr + vi * si).astype(BF16), (vi * sr - vr * si).astype(BF16)

        def away(i, carry, s=s):
            d = tiles - 1 - i
            peer = lax.rem(me_t + d, tiles)
            re, im = rows_of(peer)
            kg_send[peer, s, 0] = re
            kg_send[peer, s, 1] = im
            kg_copy(s, d).start()
            return carry

        lax.fori_loop(0, tiles - 1, away, 0)
        re, im = rows_of(me_t)
        kg_recv[me_t, s, 0] = re
        kg_recv[me_t, s, 1] = im

    for h in range(2):

        def stage(r, h=h):
            left[pl.ds(r, step), h * n : (h + 1) * n] = dot(
                back[pl.ds(h * n + r, step), :], ystack[...]
            ).astype(BF16)

        blocks(n, step, stage)

    def mk_copy(d):
        peer = lax.rem(me_z + d, zdev)
        return pltpu.make_async_remote_copy(
            src_ref=mk_send.at[peer],
            dst_ref=mk_recv.at[d - 1],
            send_sem=mk_s.at[d - 1],
            recv_sem=mk_r.at[d - 1],
            device_id={"zone": peer},
            device_id_type=MESH,
        )

    def mask_rows(peer):
        return dot(left[pl.ds(pl.multiple_of(peer * zrows, zrows), zrows), :], fore[:, :n])

    def away(i, carry):
        d = i + 1
        peer = lax.rem(me_z + d, zdev)
        mk_send[peer] = mask_rows(peer).astype(BF16)
        mk_copy(d).start()
        return carry

    lax.fori_loop(0, zdev - 1, away, 0)
    mk_own[...] = mask_rows(me_z)
    total = mk_own[...]
    for d in range(1, zdev):
        mk_copy(d).wait_recv()
        total = total + mk_recv[d - 1].astype(F32)
    mask_out[...] = total

    own_slots = pltpu.make_async_copy(kg_recv.at[me_t], kg_out.at[me_t], local_sem.at[4])
    own_slots.start()
    stores = [own_slots]
    for s in range(2):
        for d in range(1, tiles):
            kg_copy(s, d).wait_recv()
            source = lax.rem(me_t + tiles - d, tiles)
            store = pltpu.make_async_copy(
                kg_recv.at[source, s], kg_out.at[source, s], out_sem.at[s, d - 1]
            )
            store.start()
            stores.append(store)
    for store in stores:
        store.wait()
    for s in range(2):
        for d in range(1, tiles):
            panel_copy(s, d).wait_send()
            kg_copy(s, d).wait_send()
    to_sib.wait_send()
    for p in range(PIECES):
        slope_copy(p).wait_send()
        for d in range(1, chips):
            chip_copy(d, p).wait_send()
    for d in range(1, zdev):
        mk_copy(d).wait_send()


def shards(sizes, mask_levels, blend_weights, zone_pairs, kernels, resist_cot):
    tiles, zdev, n, rows, zones = sizes
    back, fore = stacked_tables(n)
    zrows = n // zdev
    chips = zdev // CORES
    half = n // CORES
    vmem = pl.BlockSpec(memory_space=pltpu.VMEM)
    anywhere = pl.BlockSpec(memory_space=pl.ANY)
    dma = pltpu.SemaphoreType.DMA
    away = max(tiles - 1, 1)
    mask_rows, returned = pl.pallas_call(
        functools.partial(kernel, sizes),
        out_shape=(
            jax.ShapeDtypeStruct((zrows, n), F32),
            jax.ShapeDtypeStruct((tiles, 2, 2, rows, n), BF16),
        ),
        in_specs=[
            pl.BlockSpec(memory_space=pltpu.SMEM),
            vmem,
            vmem,
            anywhere,
            anywhere,
            anywhere,
            anywhere,
        ],
        out_specs=(vmem, anywhere),
        scratch_shapes=[
            pltpu.VMEM((n, n), jnp.int32),
            pltpu.VMEM((n, n), F32),
            pltpu.VMEM((2 * n, 2 * n), BF16),
            pltpu.VMEM((2 * n, 2 * n), BF16),
            pltpu.VMEM((tiles, 2, 2, rows, n), BF16),
            pltpu.VMEM((2, 2, n, n), BF16),
            pltpu.VMEM((n, n), BF16),
            pltpu.VMEM((n, 2 * n), BF16),
            pltpu.VMEM((n, 2 * n), F32),
            pltpu.VMEM((2 * n, n), BF16),
            pltpu.VMEM((2, n, 2 * n), F32),
            pltpu.VMEM((n, n), F32),
            pltpu.VMEM((half, n), F32),
            pltpu.VMEM((half, n), F32),
            pltpu.VMEM((half, n), BF16),
            pltpu.VMEM((chips - 1, half, n), BF16),
            pltpu.VMEM((n, n), F32),
            pltpu.VMEM((tiles, 2, 2, rows, n), BF16),
            pltpu.VMEM((tiles, 2, 2, rows, n), BF16),
            pltpu.VMEM((n, 2 * n), F32),
            pltpu.VMEM((2 * n, n), BF16),
            pltpu.VMEM((zrows, n), F32),
            pltpu.VMEM((zdev, zrows, n), BF16),
            pltpu.VMEM((zdev - 1, zrows, n), BF16),
            dma((5,)),
            dma((2, away)),
            dma((2, away)),
            dma,
            dma,
            dma((chips - 1, PIECES)),
            dma((chips - 1, PIECES)),
            dma((PIECES,)),
            dma((PIECES,)),
            dma((2, away)),
            dma((2, away)),
            dma((zdev - 1,)),
            dma((zdev - 1,)),
            dma((2, away)),
        ],
        compiler_params=pltpu.CompilerParams(
            collective_id=0, has_side_effects=True, vmem_limit_bytes=56 * 1024 * 1024
        ),
        cost_estimate=pl.CostEstimate(
            flops=88 * n * n * n, bytes_accessed=10 * n * n * 4, transcendentals=n * n
        ),
    )(
        zone_pairs,
        blend_weights,
        kernels,
        mask_levels[0],
        resist_cot[0],
        jnp.asarray(back),
        jnp.asarray(fore),
    )
    def own_of(zone, pairs):
        owner = jnp.int32(0)
        for t in range(tiles):
            owner = jnp.where(pairs[t, 0] == zone, jnp.int32(t), owner)
        return owner

    def prior_of(zone, pairs):
        return own_of(lax.rem(zone + zones - 1, zones), pairs)

    def gather(pairs, mask_in, first, second, earlier, mask_out, kgrad_out):
        zone = pl.program_id(0)
        own, prior = own_of(zone, pairs), prior_of(zone, pairs)
        keep_own = pairs[own, 1] == pairs[own, 0]
        keep_prior = pairs[prior, 1] != pairs[prior, 0]
        value = first[0, 0].astype(F32)
        value = value + jnp.where(keep_own, second[0, 0].astype(F32), 0.0)
        value = value + jnp.where(keep_prior, earlier[0, 0].astype(F32), 0.0)
        kgrad_out[0, 0] = value

        @pl.when(zone == 0)
        def _():
            mask_out[0] = mask_in[...]

    slot = (1, 1, 2, rows, n)
    mask_grad, kernel_grad = pl.pallas_call(
        gather,
        grid_spec=pltpu.PrefetchScalarGridSpec(
            num_scalar_prefetch=1,
            grid=(zones,),
            in_specs=[
                pl.BlockSpec((zrows, n), lambda z, pairs: (0, 0)),
                pl.BlockSpec(slot, lambda z, pairs: (own_of(z, pairs), 0, 0, 0, 0)),
                pl.BlockSpec(slot, lambda z, pairs: (own_of(z, pairs), 1, 0, 0, 0)),
                pl.BlockSpec(slot, lambda z, pairs: (prior_of(z, pairs), 1, 0, 0, 0)),
            ],
            out_specs=(
                pl.BlockSpec((1, zrows, n), lambda z, pairs: (0, 0, 0)),
                pl.BlockSpec((1, 1, 2, rows, n), lambda z, pairs: (z, 0, 0, 0, 0)),
            ),
        ),
        out_shape=(
            jax.ShapeDtypeStruct((1, zrows, n), F32),
            jax.ShapeDtypeStruct((zones, 1, 2, rows, n), F32),
        ),
    )(zone_pairs, mask_rows, returned, returned, returned)
    return (mask_grad, kernel_grad)


def solution(mesh):
    placed = (
        P(("grp", "tile"), None, None),
        P(("grp", "tile"), None),
        P("grp", None),
        P(None, "zone", None, "tile", None),
        P(("grp", "tile"), None, None),
    )

    def run(mask_levels, blend_weights, zone_pairs, kernels, resist_cot):
        tiles, zdev = mesh.shape["tile"], mesh.shape["zone"]
        sizes = (
            tiles,
            zdev,
            mask_levels.shape[2],
            kernels.shape[3] // tiles,
            kernels.shape[0],
        )
        return jax.shard_map(
            functools.partial(shards, sizes),
            mesh=mesh,
            in_specs=placed,
            out_specs=(P(("grp", "tile"), "zone", None), P("grp", "zone", None, "tile", None)),
            check_vma=False,
        )(mask_levels, blend_weights, zone_pairs, kernels, resist_cot)

    return run
```

```python
import functools
import math

import jax
import jax.numpy as jnp
import ml_dtypes
import numpy as np
from jax import lax
from jax.experimental import pallas as pl
from jax.experimental.pallas import tpu as pltpu
from jax.sharding import PartitionSpec as P

LEVELS = 15
BLEND = 16
STEEP = 4.0
THRESHOLD = 1.0
F32 = jnp.float32
BF16 = jnp.bfloat16
MESH = pl.DeviceIdType.MESH
PIECES = 4
CORES = 2


def stacked_tables(length):
    index = np.arange(length, dtype=np.int64)
    angle = ((index[:, None] * index[None, :]) % length) * (2.0 * math.pi / length)
    factor = 1.0 / math.sqrt(length)
    cos = (np.cos(angle) * factor).astype(np.float32).astype(ml_dtypes.bfloat16)
    sin = (-np.sin(angle) * factor).astype(np.float32).astype(ml_dtypes.bfloat16)
    back = np.block([[cos, sin], [-sin, cos]]).astype(ml_dtypes.bfloat16)
    fore = np.block([[cos, -sin], [sin, cos]]).astype(ml_dtypes.bfloat16)
    return back, fore


def dot(left, right):
    return jnp.dot(left, right, preferred_element_type=F32)


def blocks(total, step, body):
    def one(index, carry):
        body(pl.multiple_of(index * step, step))
        return carry

    lax.fori_loop(0, total // step, one, 0)


def kernel(
    sizes,
    pairs,
    blend,
    kern,
    levels_any,
    cot_any,
    back_any,
    fore_any,
    mask_out,
    kg_out,
    levels,
    cot,
    back,
    fore,
    outgoing,
    panels,
    mvals,
    left,
    spec,
    wave,
    fields,
    image,
    sib_in,
    chip_sum,
    chip_send,
    chip_in,
    slope,
    kg_send,
    kg_recv,
    ygrad,
    ystack,
    mk_own,
    mk_send,
    mk_recv,
    local_sem,
    pan_s,
    pan_r,
    sib_s,
    sib_r,
    chip_s,
    chip_r,
    slope_s,
    slope_r,
    kg_s,
    kg_r,
    mk_s,
    mk_r,
    out_sem,
):
    tiles, zdev, length, rows, zones = sizes
    n = length
    step = n // 2
    zrows = n // zdev
    chips = zdev // CORES
    me_t = lax.axis_index("tile")
    me_z = lax.axis_index("zone")
    chip = me_z // CORES
    core = me_z % CORES
    sib = chip * CORES + (1 - core)

    loads = [
        pltpu.make_async_copy(src, dst, local_sem.at[i])
        for i, (src, dst) in enumerate(
            ((levels_any, levels), (back_any, back), (fore_any, fore), (cot_any, cot))
        )
    ]
    barrier = pltpu.get_barrier_semaphore()
    for d in range(1, tiles):
        pl.semaphore_signal(
            barrier, inc=1, device_id={"tile": lax.rem(me_t + d, tiles)}, device_id_type=MESH
        )
    for d in range(1, zdev):
        pl.semaphore_signal(
            barrier, inc=1, device_id={"zone": lax.rem(me_z + d, zdev)}, device_id_type=MESH
        )
    my_rows = pl.ds(pl.multiple_of(me_t * rows, rows), rows)
    for t in range(tiles):
        for s in range(2):
            outgoing[t, s] = kern[pairs[t, s], 0]
    for s in range(2):
        panels[s, :, my_rows, :] = kern[pairs[me_t, s], 0]
    pl.semaphore_wait(barrier, tiles + zdev - 2)

    def panel_copy(s, d):
        peer = lax.rem(me_t + d, tiles)
        return pltpu.make_async_remote_copy(
            src_ref=outgoing.at[peer, s],
            dst_ref=panels.at[s, :, my_rows, :],
            send_sem=pan_s.at[s, d - 1],
            recv_sem=pan_r.at[s, d - 1],
            device_id={"tile": peer},
            device_id_type=MESH,
        )

    for d in range(tiles - 1, 0, -1):
        panel_copy(0, d).start()
    for load in loads:
        load.start()

    first_zone, second_zone = pairs[me_t, 0], pairs[me_t, 1]
    share0 = jnp.where(first_zone != second_zone, blend[...].astype(F32) / BLEND, F32(1.0))
    shares = (share0, 1.0 - share0)

    loads[0].wait()
    mvals[...] = (2.0 * levels[...].astype(F32) / LEVELS - 1.0).astype(BF16)
    loads[1].wait()
    loads[2].wait()
    for h in range(2):

        def stage(r, h=h):
            left[pl.ds(r, step), h * n : (h + 1) * n] = dot(
                fore[pl.ds(h * n + r, step), :n], mvals[...]
            ).astype(BF16)

        blocks(n, step, stage)

    def stage(r):
        spec[pl.ds(r, step), :] = dot(left[pl.ds(r, step), :], back[...])

    blocks(n, step, stage)

    def from_left(table, h):
        def stage(r):
            left[pl.ds(r, step), h * n : (h + 1) * n] = dot(
                table[pl.ds(h * n + r, step), :], wave[...]
            ).astype(BF16)

        blocks(n, step, stage)

    half = n // CORES
    piece = half // PIECES
    to_sib = pltpu.make_async_remote_copy(
        src_ref=image.at[pl.ds(pl.multiple_of((1 - core) * half, half), half), :],
        dst_ref=sib_in,
        send_sem=sib_s,
        recv_sem=sib_r,
        device_id={"zone": sib},
        device_id_type=MESH,
    )

    for d in range(tiles - 1, 0, -1):
        panel_copy(0, d).wait_send()
        panel_copy(1, d).start()
    for s in range(2):
        for d in range(1, tiles):
            panel_copy(s, d).wait_recv()

        def stage(r, s=s):
            at = pl.ds(r, 64)
            hr, hi = panels[s, 0, at, :].astype(F32), panels[s, 1, at, :].astype(F32)
            sr, si = spec[at, :n], spec[at, n:]
            wave[at, :] = (hr * sr - hi * si).astype(BF16)
            wave[pl.ds(n + r, 64), :] = (hr * si + hi * sr).astype(BF16)

        blocks(n, 64, stage)
        from_left(back, 0)
        from_left(back, 1)

        for i in range(CORES):
            start = (1 - core) * half if i == 0 else core * half
            at = pl.ds(pl.multiple_of(start, half), half)
            e = dot(left[at, :], fore[...])
            fields[s, at, :] = e
            er, ei = e[:, :n], e[:, n:]
            term = shares[s] * (er * er + ei * ei)
            image[at, :] = term if s == 0 else image[at, :] + term
            if s == 1 and i == 0:
                to_sib.start()

    to_sib.wait_recv()

    def chip_copy(d, p):
        at = pl.ds(p * piece, piece)
        return pltpu.make_async_remote_copy(
            src_ref=chip_send.at[at, :],
            dst_ref=chip_in.at[d - 1, at, :],
            send_sem=chip_s.at[d - 1, p],
            recv_sem=chip_r.at[d - 1, p],
            device_id={"zone": lax.rem(chip + d, chips) * CORES + core},
            device_id_type=MESH,
        )

    for p in range(PIECES):
        at = pl.ds(p * piece, piece)
        here = pl.ds(pl.multiple_of(core * half + p * piece, piece), piece)
        total = image[here, :] + sib_in[at, :]
        chip_sum[at, :] = total
        chip_send[at, :] = total.astype(BF16)
        for d in range(1, chips):
            chip_copy(d, p).start()
    loads[3].wait()

    def slope_copy(p):
        here = pl.ds(pl.multiple_of(core * half + p * piece, piece), piece)
        return pltpu.make_async_remote_copy(
            src_ref=slope.at[here, :],
            dst_ref=slope.at[here, :],
            send_sem=slope_s.at[p],
            recv_sem=slope_r.at[p],
            device_id={"zone": sib},
            device_id_type=MESH,
        )

    for p in range(PIECES):
        for d in range(1, chips):
            chip_copy(d, p).wait_recv()
        at = pl.ds(p * piece, piece)
        total = chip_sum[at, :]
        for d in range(1, chips):
            total = total + chip_in[d - 1, at, :].astype(F32)
        resist = jax.nn.sigmoid(STEEP * (total - THRESHOLD))
        here = pl.ds(pl.multiple_of(core * half + p * piece, piece), piece)
        slope[here, :] = cot[here, :] * STEEP * resist * (1.0 - resist)
        slope_copy(p).start()
    for p in range(PIECES):
        slope_copy(p).wait_recv()

    def kg_copy(s, d):
        peer = lax.rem(me_t + d, tiles)
        return pltpu.make_async_remote_copy(
            src_ref=kg_send.at[peer, s],
            dst_ref=kg_recv.at[me_t, s],
            send_sem=kg_s.at[s, d - 1],
            recv_sem=kg_r.at[s, d - 1],
            device_id={"tile": peer},
            device_id_type=MESH,
        )

    for s in range(2):

        def stage(r, s=s):
            at = pl.ds(r, 64)
            scaled = 2.0 * shares[s] * slope[at, :]
            wave[at, :] = (scaled * fields[s, at, :n]).astype(BF16)
            wave[pl.ds(n + r, 64), :] = (scaled * fields[s, at, n:]).astype(BF16)

        blocks(n, 64, stage)
        from_left(fore, 0)
        from_left(fore, 1)

        def rows_of(peer, s=s):
            base = pl.multiple_of(peer * rows, rows)
            at = pl.ds(base, rows)
            v = dot(left[at, :], back[...])
            vr, vi = v[:, :n], v[:, n:]
            sr, si = spec[at, :n], spec[at, n:]
            hr, hi = panels[s, 0, at, :].astype(F32), panels[s, 1, at, :].astype(F32)
            yr = vr * hr + vi * hi
            yi = vi * hr - vr * hi
            if s == 0:
                ygrad[at, :n] = yr
                ygrad[at, n:] = yi
            else:
                ystack[at, :] = (ygrad[at, :n] + yr).astype(BF16)
                ystack[pl.ds(n + base, rows), :] = (ygrad[at, n:] + yi).astype(BF16)
            return (vr * sr + vi * si).astype(BF16), (vi * sr - vr * si).astype(BF16)

        def away(i, carry, s=s):
            d = tiles - 1 - i
            peer = lax.rem(me_t + d, tiles)
            re, im = rows_of(peer)
            kg_send[peer, s, 0] = re
            kg_send[peer, s, 1] = im
            kg_copy(s, d).start()
            return carry

        lax.fori_loop(0, tiles - 1, away, 0)
        re, im = rows_of(me_t)
        kg_recv[me_t, s, 0] = re
        kg_recv[me_t, s, 1] = im

    for h in range(2):

        def stage(r, h=h):
            left[pl.ds(r, step), h * n : (h + 1) * n] = dot(
                back[pl.ds(h * n + r, step), :], ystack[...]
            ).astype(BF16)

        blocks(n, step, stage)

    def mk_copy(d):
        peer = lax.rem(me_z + d, zdev)
        return pltpu.make_async_remote_copy(
            src_ref=mk_send.at[peer],
            dst_ref=mk_recv.at[d - 1],
            send_sem=mk_s.at[d - 1],
            recv_sem=mk_r.at[d - 1],
            device_id={"zone": peer},
            device_id_type=MESH,
        )

    def mask_rows(peer):
        return dot(left[pl.ds(pl.multiple_of(peer * zrows, zrows), zrows), :], fore[:, :n])

    def away(i, carry):
        d = i + 1
        peer = lax.rem(me_z + d, zdev)
        mk_send[peer] = mask_rows(peer).astype(BF16)
        mk_copy(d).start()
        return carry

    lax.fori_loop(0, zdev - 1, away, 0)
    mk_own[...] = mask_rows(me_z)
    total = mk_own[...]
    for d in range(1, zdev):
        mk_copy(d).wait_recv()
        total = total + mk_recv[d - 1].astype(F32)
    mask_out[...] = total

    own_slots = pltpu.make_async_copy(kg_recv.at[me_t], kg_out.at[me_t], local_sem.at[4])
    own_slots.start()
    stores = [own_slots]
    for s in range(2):
        for d in range(1, tiles):
            kg_copy(s, d).wait_recv()
            source = lax.rem(me_t + tiles - d, tiles)
            store = pltpu.make_async_copy(
                kg_recv.at[source, s], kg_out.at[source, s], out_sem.at[s, d - 1]
            )
            store.start()
            stores.append(store)
    for store in stores:
        store.wait()
    for s in range(2):
        for d in range(1, tiles):
            kg_copy(s, d).wait_send()
    for d in range(1, tiles):
        panel_copy(1, d).wait_send()
    to_sib.wait_send()
    for p in range(PIECES):
        slope_copy(p).wait_send()
        for d in range(1, chips):
            chip_copy(d, p).wait_send()
    for d in range(1, zdev):
        mk_copy(d).wait_send()


def shards(sizes, mask_levels, blend_weights, zone_pairs, kernels, resist_cot):
    tiles, zdev, n, rows, zones = sizes
    back, fore = stacked_tables(n)
    zrows = n // zdev
    chips = zdev // CORES
    half = n // CORES
    vmem = pl.BlockSpec(memory_space=pltpu.VMEM)
    anywhere = pl.BlockSpec(memory_space=pl.ANY)
    dma = pltpu.SemaphoreType.DMA
    away = max(tiles - 1, 1)
    mask_rows, returned = pl.pallas_call(
        functools.partial(kernel, sizes),
        out_shape=(
            jax.ShapeDtypeStruct((zrows, n), F32),
            jax.ShapeDtypeStruct((tiles, 2, 2, rows, n), BF16),
        ),
        in_specs=[
            pl.BlockSpec(memory_space=pltpu.SMEM),
            vmem,
            vmem,
            anywhere,
            anywhere,
            anywhere,
            anywhere,
        ],
        out_specs=(vmem, anywhere),
        scratch_shapes=[
            pltpu.VMEM((n, n), jnp.int32),
            pltpu.VMEM((n, n), F32),
            pltpu.VMEM((2 * n, 2 * n), BF16),
            pltpu.VMEM((2 * n, 2 * n), BF16),
            pltpu.VMEM((tiles, 2, 2, rows, n), BF16),
            pltpu.VMEM((2, 2, n, n), BF16),
            pltpu.VMEM((n, n), BF16),
            pltpu.VMEM((n, 2 * n), BF16),
            pltpu.VMEM((n, 2 * n), F32),
            pltpu.VMEM((2 * n, n), BF16),
            pltpu.VMEM((2, n, 2 * n), F32),
            pltpu.VMEM((n, n), F32),
            pltpu.VMEM((half, n), F32),
            pltpu.VMEM((half, n), F32),
            pltpu.VMEM((half, n), BF16),
            pltpu.VMEM((chips - 1, half, n), BF16),
            pltpu.VMEM((n, n), F32),
            pltpu.VMEM((tiles, 2, 2, rows, n), BF16),
            pltpu.VMEM((tiles, 2, 2, rows, n), BF16),
            pltpu.VMEM((n, 2 * n), F32),
            pltpu.VMEM((2 * n, n), BF16),
            pltpu.VMEM((zrows, n), F32),
            pltpu.VMEM((zdev, zrows, n), BF16),
            pltpu.VMEM((zdev - 1, zrows, n), BF16),
            dma((5,)),
            dma((2, away)),
            dma((2, away)),
            dma,
            dma,
            dma((chips - 1, PIECES)),
            dma((chips - 1, PIECES)),
            dma((PIECES,)),
            dma((PIECES,)),
            dma((2, away)),
            dma((2, away)),
            dma((zdev - 1,)),
            dma((zdev - 1,)),
            dma((2, away)),
        ],
        compiler_params=pltpu.CompilerParams(
            collective_id=0, has_side_effects=True, vmem_limit_bytes=56 * 1024 * 1024
        ),
        cost_estimate=pl.CostEstimate(
            flops=88 * n * n * n, bytes_accessed=10 * n * n * 4, transcendentals=n * n
        ),
    )(
        zone_pairs,
        blend_weights,
        kernels,
        mask_levels[0],
        resist_cot[0],
        jnp.asarray(back),
        jnp.asarray(fore),
    )
    def own_of(zone, pairs):
        owner = jnp.int32(0)
        for t in range(tiles):
            owner = jnp.where(pairs[t, 0] == zone, jnp.int32(t), owner)
        return owner

    def gather(pairs, mask_in, got, mask_out, kgrad_out):
        mask_out[0] = mask_in[...]
        for zone in range(zones):
            own, prior = own_of(zone, pairs), own_of((zone - 1) % zones, pairs)
            keep_own = pairs[own, 1] == pairs[own, 0]
            keep_prior = pairs[prior, 1] != pairs[prior, 0]
            for c in range(2):
                value = got[own, 0, c].astype(F32)
                value = value + jnp.where(keep_own, got[own, 1, c].astype(F32), 0.0)
                value = value + jnp.where(keep_prior, got[prior, 1, c].astype(F32), 0.0)
                kgrad_out[zone, 0, c] = value

    mask_grad, kernel_grad = pl.pallas_call(
        gather,
        in_specs=[pl.BlockSpec(memory_space=pltpu.SMEM), vmem, vmem],
        out_specs=(vmem, vmem),
        out_shape=(
            jax.ShapeDtypeStruct((1, zrows, n), F32),
            jax.ShapeDtypeStruct((zones, 1, 2, rows, n), F32),
        ),
        compiler_params=pltpu.CompilerParams(vmem_limit_bytes=60 * 1024 * 1024),
    )(zone_pairs, mask_rows, returned)
    return (mask_grad, kernel_grad)


def solution(mesh):
    placed = (
        P(("grp", "tile"), None, None),
        P(("grp", "tile"), None),
        P("grp", None),
        P(None, "zone", None, "tile", None),
        P(("grp", "tile"), None, None),
    )

    def run(mask_levels, blend_weights, zone_pairs, kernels, resist_cot):
        tiles, zdev = mesh.shape["tile"], mesh.shape["zone"]
        sizes = (
            tiles,
            zdev,
            mask_levels.shape[2],
            kernels.shape[3] // tiles,
            kernels.shape[0],
        )
        return jax.shard_map(
            functools.partial(shards, sizes),
            mesh=mesh,
            in_specs=placed,
            out_specs=(P(("grp", "tile"), "zone", None), P("grp", "zone", None, "tile", None)),
            check_vma=False,
        )(mask_levels, blend_weights, zone_pairs, kernels, resist_cot)

    return run
```

```python
import functools
import math

import jax
import jax.numpy as jnp
import ml_dtypes
import numpy as np
from jax import lax
from jax.experimental import pallas as pl
from jax.experimental.pallas import tpu as pltpu
from jax.sharding import PartitionSpec as P

LEVELS = 15
BLEND = 16
STEEP = 4.0
THRESHOLD = 1.0
F32 = jnp.float32
BF16 = jnp.bfloat16
MESH = pl.DeviceIdType.MESH
PIECES = 2
CORES = 2


def stacked_tables(length):
    index = np.arange(length, dtype=np.int64)
    angle = ((index[:, None] * index[None, :]) % length) * (2.0 * math.pi / length)
    factor = 1.0 / math.sqrt(length)
    cos = (np.cos(angle) * factor).astype(np.float32).astype(ml_dtypes.bfloat16)
    sin = (-np.sin(angle) * factor).astype(np.float32).astype(ml_dtypes.bfloat16)
    back = np.block([[cos, sin], [-sin, cos]]).astype(ml_dtypes.bfloat16)
    fore = np.block([[cos, -sin], [sin, cos]]).astype(ml_dtypes.bfloat16)
    return back, fore


def dot(left, right):
    return jnp.dot(left, right, preferred_element_type=F32)


def blocks(total, step, body):
    def one(index, carry):
        body(pl.multiple_of(index * step, step))
        return carry

    lax.fori_loop(0, total // step, one, 0)


def kernel(
    sizes,
    pairs,
    blend,
    kern,
    levels_any,
    cot_any,
    back_any,
    fore_any,
    mask_out,
    kg_out,
    levels,
    cot,
    back,
    fore,
    outgoing,
    panels,
    mvals,
    left,
    spec,
    wave,
    fields,
    image,
    sib_in,
    chip_sum,
    chip_send,
    chip_in,
    slope,
    kg_send,
    kg_recv,
    ygrad,
    ystack,
    mk_own,
    mk_send,
    mk_recv,
    local_sem,
    pan_s,
    pan_r,
    sib_s,
    sib_r,
    chip_s,
    chip_r,
    slope_s,
    slope_r,
    kg_s,
    kg_r,
    mk_s,
    mk_r,
    out_sem,
):
    tiles, zdev, length, rows, zones = sizes
    n = length
    step = n // 2
    zrows = n // zdev
    chips = zdev // CORES
    me_t = lax.axis_index("tile")
    me_z = lax.axis_index("zone")
    chip = me_z // CORES
    core = me_z % CORES
    sib = chip * CORES + (1 - core)

    loads = [
        pltpu.make_async_copy(src, dst, local_sem.at[i])
        for i, (src, dst) in enumerate(
            ((levels_any, levels), (back_any, back), (fore_any, fore), (cot_any, cot))
        )
    ]
    barrier = pltpu.get_barrier_semaphore()
    for d in range(1, tiles):
        pl.semaphore_signal(
            barrier, inc=1, device_id={"tile": lax.rem(me_t + d, tiles)}, device_id_type=MESH
        )
    for d in range(1, zdev):
        pl.semaphore_signal(
            barrier, inc=1, device_id={"zone": lax.rem(me_z + d, zdev)}, device_id_type=MESH
        )
    my_rows = pl.ds(pl.multiple_of(me_t * rows, rows), rows)
    for t in range(tiles):
        for s in range(2):
            outgoing[t, s] = kern[pairs[t, s], 0]
    for s in range(2):
        panels[s, :, my_rows, :] = kern[pairs[me_t, s], 0]
    pl.semaphore_wait(barrier, tiles + zdev - 2)

    def panel_copy(s, d):
        peer = lax.rem(me_t + d, tiles)
        return pltpu.make_async_remote_copy(
            src_ref=outgoing.at[peer, s],
            dst_ref=panels.at[s, :, my_rows, :],
            send_sem=pan_s.at[s, d - 1],
            recv_sem=pan_r.at[s, d - 1],
            device_id={"tile": peer},
            device_id_type=MESH,
        )

    for d in range(tiles - 1, 0, -1):
        panel_copy(0, d).start()
    for load in loads:
        load.start()

    first_zone, second_zone = pairs[me_t, 0], pairs[me_t, 1]
    share0 = jnp.where(first_zone != second_zone, blend[...].astype(F32) / BLEND, F32(1.0))
    shares = (share0, 1.0 - share0)

    loads[0].wait()
    mvals[...] = (2.0 * levels[...].astype(F32) / LEVELS - 1.0).astype(BF16)
    loads[1].wait()
    loads[2].wait()
    for h in range(2):

        def stage(r, h=h):
            left[pl.ds(r, step), h * n : (h + 1) * n] = dot(
                fore[pl.ds(h * n + r, step), :n], mvals[...]
            ).astype(BF16)

        blocks(n, step, stage)

    def stage(r):
        spec[pl.ds(r, step), :] = dot(left[pl.ds(r, step), :], back[...])

    blocks(n, step, stage)

    def from_left(table, h):
        def stage(r):
            left[pl.ds(r, step), h * n : (h + 1) * n] = dot(
                table[pl.ds(h * n + r, step), :], wave[...]
            ).astype(BF16)

        blocks(n, step, stage)

    half = n // CORES
    piece = half // PIECES
    to_sib = pltpu.make_async_remote_copy(
        src_ref=image.at[pl.ds(pl.multiple_of((1 - core) * half, half), half), :],
        dst_ref=sib_in,
        send_sem=sib_s,
        recv_sem=sib_r,
        device_id={"zone": sib},
        device_id_type=MESH,
    )

    for d in range(tiles - 1, 0, -1):
        panel_copy(0, d).wait_send()
        panel_copy(1, d).start()
    for s in range(2):
        for d in range(1, tiles):
            panel_copy(s, d).wait_recv()

        def stage(r, s=s):
            at = pl.ds(r, 64)
            hr, hi = panels[s, 0, at, :].astype(F32), panels[s, 1, at, :].astype(F32)
            sr, si = spec[at, :n], spec[at, n:]
            wave[at, :] = (hr * sr - hi * si).astype(BF16)
            wave[pl.ds(n + r, 64), :] = (hr * si + hi * sr).astype(BF16)

        blocks(n, 64, stage)
        from_left(back, 0)
        from_left(back, 1)

        for i in range(CORES):
            start = (1 - core) * half if i == 0 else core * half
            at = pl.ds(pl.multiple_of(start, half), half)
            e = dot(left[at, :], fore[...])
            fields[s, at, :] = e
            er, ei = e[:, :n], e[:, n:]
            term = shares[s] * (er * er + ei * ei)
            image[at, :] = term if s == 0 else image[at, :] + term
            if s == 1 and i == 0:
                to_sib.start()

    to_sib.wait_recv()

    def chip_copy(d, p):
        at = pl.ds(p * piece, piece)
        return pltpu.make_async_remote_copy(
            src_ref=chip_send.at[at, :],
            dst_ref=chip_in.at[d - 1, at, :],
            send_sem=chip_s.at[d - 1, p],
            recv_sem=chip_r.at[d - 1, p],
            device_id={"zone": lax.rem(chip + d, chips) * CORES + core},
            device_id_type=MESH,
        )

    for p in range(PIECES):
        at = pl.ds(p * piece, piece)
        here = pl.ds(pl.multiple_of(core * half + p * piece, piece), piece)
        total = image[here, :] + sib_in[at, :]
        chip_sum[at, :] = total
        chip_send[at, :] = total.astype(BF16)
        for d in range(1, chips):
            chip_copy(d, p).start()
    loads[3].wait()

    def slope_copy(p):
        here = pl.ds(pl.multiple_of(core * half + p * piece, piece), piece)
        return pltpu.make_async_remote_copy(
            src_ref=slope.at[here, :],
            dst_ref=slope.at[here, :],
            send_sem=slope_s.at[p],
            recv_sem=slope_r.at[p],
            device_id={"zone": sib},
            device_id_type=MESH,
        )

    for p in range(PIECES):
        for d in range(1, chips):
            chip_copy(d, p).wait_recv()
        at = pl.ds(p * piece, piece)
        total = chip_sum[at, :]
        for d in range(1, chips):
            total = total + chip_in[d - 1, at, :].astype(F32)
        resist = jax.nn.sigmoid(STEEP * (total - THRESHOLD))
        here = pl.ds(pl.multiple_of(core * half + p * piece, piece), piece)
        slope[here, :] = cot[here, :] * STEEP * resist * (1.0 - resist)
        slope_copy(p).start()
    for p in range(PIECES):
        slope_copy(p).wait_recv()

    def kg_copy(s, d):
        peer = lax.rem(me_t + d, tiles)
        return pltpu.make_async_remote_copy(
            src_ref=kg_send.at[peer, s],
            dst_ref=kg_recv.at[me_t, s],
            send_sem=kg_s.at[s, d - 1],
            recv_sem=kg_r.at[s, d - 1],
            device_id={"tile": peer},
            device_id_type=MESH,
        )

    for s in range(2):

        def stage(r, s=s):
            at = pl.ds(r, 64)
            scaled = 2.0 * shares[s] * slope[at, :]
            wave[at, :] = (scaled * fields[s, at, :n]).astype(BF16)
            wave[pl.ds(n + r, 64), :] = (scaled * fields[s, at, n:]).astype(BF16)

        blocks(n, 64, stage)
        from_left(fore, 0)
        from_left(fore, 1)

        def rows_of(peer, s=s):
            base = pl.multiple_of(peer * rows, rows)
            at = pl.ds(base, rows)
            v = dot(left[at, :], back[...])
            vr, vi = v[:, :n], v[:, n:]
            sr, si = spec[at, :n], spec[at, n:]
            hr, hi = panels[s, 0, at, :].astype(F32), panels[s, 1, at, :].astype(F32)
            yr = vr * hr + vi * hi
            yi = vi * hr - vr * hi
            if s == 0:
                ygrad[at, :n] = yr
                ygrad[at, n:] = yi
            else:
                ystack[at, :] = (ygrad[at, :n] + yr).astype(BF16)
                ystack[pl.ds(n + base, rows), :] = (ygrad[at, n:] + yi).astype(BF16)
            return (vr * sr + vi * si).astype(BF16), (vi * sr - vr * si).astype(BF16)

        def away(i, carry, s=s):
            d = (tiles // 2 + i - 1) % (tiles - 1) + 1
            peer = lax.rem(me_t + d, tiles)
            re, im = rows_of(peer)
            kg_send[peer, s, 0] = re
            kg_send[peer, s, 1] = im
            kg_copy(s, d).start()
            return carry

        lax.fori_loop(0, tiles - 1, away, 0)
        re, im = rows_of(me_t)
        kg_recv[me_t, s, 0] = re
        kg_recv[me_t, s, 1] = im

    for h in range(2):

        def stage(r, h=h):
            left[pl.ds(r, step), h * n : (h + 1) * n] = dot(
                back[pl.ds(h * n + r, step), :], ystack[...]
            ).astype(BF16)

        blocks(n, step, stage)

    def mk_copy(d):
        peer = lax.rem(me_z + d, zdev)
        return pltpu.make_async_remote_copy(
            src_ref=mk_send.at[peer],
            dst_ref=mk_recv.at[d - 1],
            send_sem=mk_s.at[d - 1],
            recv_sem=mk_r.at[d - 1],
            device_id={"zone": peer},
            device_id_type=MESH,
        )

    def mask_rows(peer):
        return dot(left[pl.ds(pl.multiple_of(peer * zrows, zrows), zrows), :], fore[:, :n])

    def away(i, carry):
        d = i + 1
        peer = lax.rem(me_z + d, zdev)
        mk_send[peer] = mask_rows(peer).astype(BF16)
        mk_copy(d).start()
        return carry

    lax.fori_loop(0, zdev - 1, away, 0)
    mk_own[...] = mask_rows(me_z)
    total = mk_own[...]
    for d in range(1, zdev):
        mk_copy(d).wait_recv()
        total = total + mk_recv[d - 1].astype(F32)
    mask_out[...] = total

    own_slots = pltpu.make_async_copy(kg_recv.at[me_t], kg_out.at[me_t], local_sem.at[4])
    own_slots.start()
    stores = [own_slots]
    for s in range(2):
        for d in range(1, tiles):
            kg_copy(s, d).wait_recv()
            source = lax.rem(me_t + tiles - d, tiles)
            store = pltpu.make_async_copy(
                kg_recv.at[source, s], kg_out.at[source, s], out_sem.at[s, d - 1]
            )
            store.start()
            stores.append(store)
    for store in stores:
        store.wait()
    for s in range(2):
        for d in range(1, tiles):
            kg_copy(s, d).wait_send()
    for d in range(1, tiles):
        panel_copy(1, d).wait_send()
    to_sib.wait_send()
    for p in range(PIECES):
        slope_copy(p).wait_send()
        for d in range(1, chips):
            chip_copy(d, p).wait_send()
    for d in range(1, zdev):
        mk_copy(d).wait_send()


def shards(sizes, mask_levels, blend_weights, zone_pairs, kernels, resist_cot):
    tiles, zdev, n, rows, zones = sizes
    back, fore = stacked_tables(n)
    zrows = n // zdev
    chips = zdev // CORES
    half = n // CORES
    vmem = pl.BlockSpec(memory_space=pltpu.VMEM)
    anywhere = pl.BlockSpec(memory_space=pl.ANY)
    dma = pltpu.SemaphoreType.DMA
    away = max(tiles - 1, 1)
    mask_rows, returned = pl.pallas_call(
        functools.partial(kernel, sizes),
        out_shape=(
            jax.ShapeDtypeStruct((zrows, n), F32),
            jax.ShapeDtypeStruct((tiles, 2, 2, rows, n), BF16),
        ),
        in_specs=[
            pl.BlockSpec(memory_space=pltpu.SMEM),
            vmem,
            vmem,
            anywhere,
            anywhere,
            anywhere,
            anywhere,
        ],
        out_specs=(vmem, anywhere),
        scratch_shapes=[
            pltpu.VMEM((n, n), jnp.int32),
            pltpu.VMEM((n, n), F32),
            pltpu.VMEM((2 * n, 2 * n), BF16),
            pltpu.VMEM((2 * n, 2 * n), BF16),
            pltpu.VMEM((tiles, 2, 2, rows, n), BF16),
            pltpu.VMEM((2, 2, n, n), BF16),
            pltpu.VMEM((n, n), BF16),
            pltpu.VMEM((n, 2 * n), BF16),
            pltpu.VMEM((n, 2 * n), F32),
            pltpu.VMEM((2 * n, n), BF16),
            pltpu.VMEM((2, n, 2 * n), F32),
            pltpu.VMEM((n, n), F32),
            pltpu.VMEM((half, n), F32),
            pltpu.VMEM((half, n), F32),
            pltpu.VMEM((half, n), BF16),
            pltpu.VMEM((chips - 1, half, n), BF16),
            pltpu.VMEM((n, n), F32),
            pltpu.VMEM((tiles, 2, 2, rows, n), BF16),
            pltpu.VMEM((tiles, 2, 2, rows, n), BF16),
            pltpu.VMEM((n, 2 * n), F32),
            pltpu.VMEM((2 * n, n), BF16),
            pltpu.VMEM((zrows, n), F32),
            pltpu.VMEM((zdev, zrows, n), BF16),
            pltpu.VMEM((zdev - 1, zrows, n), BF16),
            dma((5,)),
            dma((2, away)),
            dma((2, away)),
            dma,
            dma,
            dma((chips - 1, PIECES)),
            dma((chips - 1, PIECES)),
            dma((PIECES,)),
            dma((PIECES,)),
            dma((2, away)),
            dma((2, away)),
            dma((zdev - 1,)),
            dma((zdev - 1,)),
            dma((2, away)),
        ],
        compiler_params=pltpu.CompilerParams(
            collective_id=0, has_side_effects=True, vmem_limit_bytes=56 * 1024 * 1024
        ),
        cost_estimate=pl.CostEstimate(
            flops=88 * n * n * n, bytes_accessed=10 * n * n * 4, transcendentals=n * n
        ),
    )(
        zone_pairs,
        blend_weights,
        kernels,
        mask_levels[0],
        resist_cot[0],
        jnp.asarray(back),
        jnp.asarray(fore),
    )
    def own_of(zone, pairs):
        owner = jnp.int32(0)
        for t in range(tiles):
            owner = jnp.where(pairs[t, 0] == zone, jnp.int32(t), owner)
        return owner

    def gather(pairs, mask_in, got, mask_out, kgrad_out):
        mask_out[0] = mask_in[...]
        for zone in range(zones):
            own, prior = own_of(zone, pairs), own_of((zone - 1) % zones, pairs)
            keep_own = pairs[own, 1] == pairs[own, 0]
            keep_prior = pairs[prior, 1] != pairs[prior, 0]
            for c in range(2):
                value = got[own, 0, c].astype(F32)
                value = value + jnp.where(keep_own, got[own, 1, c].astype(F32), 0.0)
                value = value + jnp.where(keep_prior, got[prior, 1, c].astype(F32), 0.0)
                kgrad_out[zone, 0, c] = value

    mask_grad, kernel_grad = pl.pallas_call(
        gather,
        in_specs=[pl.BlockSpec(memory_space=pltpu.SMEM), vmem, vmem],
        out_specs=(vmem, vmem),
        out_shape=(
            jax.ShapeDtypeStruct((1, zrows, n), F32),
            jax.ShapeDtypeStruct((zones, 1, 2, rows, n), F32),
        ),
        compiler_params=pltpu.CompilerParams(vmem_limit_bytes=60 * 1024 * 1024),
    )(zone_pairs, mask_rows, returned)
    return (mask_grad, kernel_grad)


def solution(mesh):
    placed = (
        P(("grp", "tile"), None, None),
        P(("grp", "tile"), None),
        P("grp", None),
        P(None, "zone", None, "tile", None),
        P(("grp", "tile"), None, None),
    )

    def run(mask_levels, blend_weights, zone_pairs, kernels, resist_cot):
        tiles, zdev = mesh.shape["tile"], mesh.shape["zone"]
        sizes = (
            tiles,
            zdev,
            mask_levels.shape[2],
            kernels.shape[3] // tiles,
            kernels.shape[0],
        )
        return jax.shard_map(
            functools.partial(shards, sizes),
            mesh=mesh,
            in_specs=placed,
            out_specs=(P(("grp", "tile"), "zone", None), P("grp", "zone", None, "tile", None)),
            check_vma=False,
        )(mask_levels, blend_weights, zone_pairs, kernels, resist_cot)

    return run
```
